32 devices in a mesh: prefix: 4 (over y, x), cand: 8 (over z, core).
Axes of the slice: x: 2, y: 2, z: 4, core: 2. Of those that a mesh axis runs over, the one named last changes fastest.
Arguments:
- query: bfloat16 [2048, 8192], P('cand', 'prefix'), may hold values from -100 to 100
- grad_out: bfloat16 [2048, 8192], P('cand', 'prefix'), may hold values from -24 to 24
- continuation_key: bfloat16 [2048, 1024], P('cand', 'prefix'), may hold values from -8 to 8
- continuation_value: bfloat16 [2048, 1024], P('cand', 'prefix'), may hold values from -6 to 6
- prompt_key: bfloat16 [768, 1024], P(('prefix', 'cand')), may hold values from -4 to 4
- shared_prompt_value: bfloat16 [768, 1024], P(('prefix', 'cand')), may hold values from -6 to 6
- assign: int32 [32], replicated, may hold values from 0 to 7, as said below
- lengths: int32 [32], replicated, may hold values from 1 to 64, as said below
- offsets: int32 [32], replicated, may hold values from 384 to 768
Outputs:
- query_grad: bfloat16 [2048, 8192], P('cand', 'prefix')
- cont_key_grad: bfloat16 [2048, 1024], P('cand', 'prefix')
- cont_value_grad: bfloat16 [2048, 1024], P('cand', 'prefix')
- prompt_key_grad: bfloat16 [768, 1024], P(('prefix', 'cand'))
- prompt_value_grad: bfloat16 [768, 1024], P(('prefix', 'cand'))
The draws below stay inside these ranges and needn't reach their ends.
Inputs may be any that keep to these rules, and one draw needn't show every extreme that they name: `assign`: each index of cand is named by exactly 4 candidates. The lengths of the candidates on one index of cand sum to at most 256; on some index they sum to exactly 256, each of its candidates having length 64.
All inputs are finite; a program needn't handle non-finite values.
Results may differ from the reference program's by a relative error of at most 0.015.
Values may be sent and summed in bfloat16 or wider, within the bound.
No kernel may reach another device: no remote copies, remote signals or barrier semaphores. Data moves between devices by JAX's collectives and lax.ppermute only.
A program may use at most 64 MiB of HBM per device.

```python
import math
import jax
import jax.numpy as jnp
from jax import lax

QUERY_HEAD_COUNT = 64
KEY_VALUE_HEADS = 8
HEAD_WIDTH = 128
CPD = 4
NCAND = 32
ROWS_DEV = 256
CONT_ROW_SLOTS = 2048
PROMPT_TOKENS = 768
N_CAND = 8


def layout_draw(key):
    device_count = NCAND // CPD
    cand_order = jax.random.permutation(jax.random.fold_in(key, 81), NCAND)
    assign = (cand_order // CPD).astype(jnp.int32)
    length_cap = ROWS_DEV // CPD
    drawn = jax.random.randint(jax.random.fold_in(key, 82), (NCAND,), 1, length_cap + 1)
    full_device = jax.random.randint(jax.random.fold_in(key, 83), (), 0, device_count)
    lengths = jnp.where(assign == full_device, length_cap, drawn).astype(jnp.int32)
    return (assign, lengths)


def draw_assign(key, part):
    return layout_draw(key)[0]


def draw_lengths(key, part):
    return layout_draw(key)[1]


def draw_offsets(key, part):
    lowest = PROMPT_TOKENS // 2
    drawn = jax.random.randint(jax.random.fold_in(key, 91), (NCAND,), lowest, PROMPT_TOKENS + 1)
    chosen = jax.random.permutation(jax.random.fold_in(key, 92), NCAND)
    cand_index = jnp.arange(NCAND)
    drawn = jnp.where(cand_index == chosen[0], PROMPT_TOKENS, drawn)
    drawn = jnp.where(cand_index == chosen[1], lowest, drawn)
    return drawn.astype(jnp.int32)


def draw_prompt_key(key, part):
    starting_sample = jax.random.truncated_normal(jax.random.fold_in(key, 72), -4.0, 4.0, (PROMPT_TOKENS, KEY_VALUE_HEADS * HEAD_WIDTH), jnp.float32)
    return starting_sample.astype(jnp.bfloat16)


def draw_query(key, part):
    starting_sample = 2.0 * jax.random.truncated_normal(jax.random.fold_in(key, 73), -4.0, 4.0, (CONT_ROW_SLOTS, QUERY_HEAD_COUNT * HEAD_WIDTH), jnp.float32)
    return starting_sample.astype(jnp.bfloat16)


def block_scale(stream_key, shape, pieces, least, largest):
    level = 1.0
    for position, shards_of in pieces:
        heights = jax.random.uniform(jax.random.fold_in(jax.random.fold_in(stream_key, 6), position), (shards_of,), jnp.float32, least / len(pieces), largest / len(pieces))
        level = level * jnp.repeat(jnp.exp(heights), shape[position] // shards_of).reshape((-1,) + (1,) * (len(shape) - 1 - position))
    return level


def normal_values(own_key, shape, scale, limit, cuts=(), held_as=jnp.bfloat16):
    values = scale * jax.random.normal(own_key, shape, jnp.float32)
    if cuts:
        values = values * block_scale(own_key, shape, cuts, -0.22, 0.18)
    return jnp.clip(values, -limit, limit).astype(held_as)


def setup_inputs(seed: int = 0) -> dict:
    splits = jax.random.split(jax.random.key(seed), 10)
    query = draw_query(jax.random.fold_in(splits[9], 71), 0)
    grad_out = normal_values(splits[1], (CONT_ROW_SLOTS, QUERY_HEAD_COUNT * HEAD_WIDTH), 4.0, 24.0, ((0, 8), (1, 4)))
    continuation_key = normal_values(splits[2], (CONT_ROW_SLOTS, KEY_VALUE_HEADS * HEAD_WIDTH), 1.5, 8.0, ((0, 8), (1, 4)))
    continuation_value = normal_values(splits[3], (CONT_ROW_SLOTS, KEY_VALUE_HEADS * HEAD_WIDTH), 1.0, 6.0, ((0, 8), (1, 4)))
    prompt_key = draw_prompt_key(jax.random.fold_in(splits[9], 71), 0)
    shared_prompt_value = normal_values(splits[5], (PROMPT_TOKENS, KEY_VALUE_HEADS * HEAD_WIDTH), 1.0, 6.0, ((0, 32),))
    assign = draw_assign(jax.random.fold_in(splits[9], 71), 0)
    lengths = draw_lengths(jax.random.fold_in(splits[9], 71), 0)
    offsets = draw_offsets(jax.random.fold_in(splits[9], 71), 0)
    return dict(query=query, grad_out=grad_out, continuation_key=continuation_key, continuation_value=continuation_value, prompt_key=prompt_key, shared_prompt_value=shared_prompt_value, assign=assign, lengths=lengths, offsets=offsets)


MASKED_SCORE = -1e+30
HIGHEST = lax.Precision.HIGHEST

def slot_layout(assign, lengths, offsets, device, slot_count):
    cand_count = assign.shape[0]
    cand_order = jnp.arange(cand_count, dtype=jnp.int32)
    earlier_same = (assign[:, None] == assign[None, :]) & (cand_order[None, :] < cand_order[:, None])
    starts = lax.optimization_barrier(jnp.sum(jnp.where(earlier_same, lengths[None, :], 0), axis=1)).astype(jnp.int32)
    slot_index = jnp.arange(slot_count, dtype=jnp.int32)
    slot_match = (assign[:, None] == device) & (slot_index[None, :] >= starts[:, None]) & (slot_index[None, :] < (starts + lengths)[:, None])
    row_valid = jnp.any(slot_match, axis=0)
    row_segment = lax.optimization_barrier(jnp.sum(jnp.where(slot_match, cand_order[:, None], 0), axis=0)).astype(jnp.int32)
    offset_row = lax.optimization_barrier(jnp.sum(jnp.where(slot_match, offsets[:, None], 0), axis=0)).astype(jnp.int32)
    return (row_valid, row_segment, offset_row)

def attend(queries, grad_rows, joined_keys, joined_values, key_segment, key_position, row_valid, row_segment, offset_row):
    row_count = queries.shape[0]
    head_count = joined_keys.shape[1]
    head_size = joined_keys.shape[2]
    key_count = joined_keys.shape[0]
    block_size = math.gcd(key_count, 256)
    block_count = key_count // block_size
    score_scale = 1.0 / math.sqrt(head_size)
    query_heads = queries.reshape(row_count, head_count, -1, head_size).astype(jnp.float32)
    grad_heads = grad_rows.reshape(query_heads.shape).astype(jnp.float32)
    slot_index = jnp.arange(row_count, dtype=jnp.int32)
    stacked = (joined_keys.reshape(block_count, block_size, head_count, head_size), joined_values.reshape(block_count, block_size, head_count, head_size), key_segment.reshape(block_count, block_size), key_position.reshape(block_count, block_size))

    def scores(block_items):
        key_block, value_block, block_segment, block_position = block_items
        prompt_ok = (block_segment[None, :] == -1) & (block_position[None, :] < offset_row[:, None])
        cont_ok = (block_segment[None, :] == row_segment[:, None]) & (block_position[None, :] <= slot_index[:, None])
        visible_mask = (row_valid[:, None] & (prompt_ok | cont_ok))[None, None]
        raw_scores = jnp.einsum('rhgd,jhd->hgrj', query_heads, key_block.astype(jnp.float32), precision=HIGHEST) * score_scale
        return (raw_scores, visible_mask)

    def normaliser(state_pair, block_items):
        running_max, summed = state_pair
        raw_scores, visible_mask = scores(block_items)
        fresh_max = jnp.maximum(running_max, lax.optimization_barrier(jnp.max(jnp.where(visible_mask, raw_scores, MASKED_SCORE), axis=3)))
        summed = summed * jnp.exp(running_max - fresh_max) + lax.optimization_barrier(jnp.sum(jnp.where(visible_mask, jnp.exp(raw_scores - fresh_max[..., None]), 0.0), axis=3))
        return ((fresh_max, summed), None)
    stat_shape = (head_count, query_heads.shape[2], row_count)
    start_pair = (jnp.full(stat_shape, MASKED_SCORE, jnp.float32), jnp.zeros(stat_shape, jnp.float32))
    (running_max, summed), _ = lax.scan(normaliser, start_pair, stacked)
    lse = running_max + jnp.log(jnp.where(row_valid[None, None, :], summed, 1.0))

    def weighting(raw_scores, visible_mask):
        return jnp.where(visible_mask, jnp.exp(raw_scores - lse[..., None]), 0.0)

    def forward(attended, block_items):
        raw_scores, visible_mask = scores(block_items)
        probs_bf = weighting(raw_scores, visible_mask).astype(jnp.bfloat16).astype(jnp.float32)
        value_block = block_items[1].astype(jnp.float32)
        return (attended + jnp.einsum('hgrj,jhd->rhgd', probs_bf, value_block, precision=HIGHEST), None)
    attended, _ = lax.scan(forward, jnp.zeros(query_heads.shape, jnp.float32), stacked)
    row_delta = jnp.transpose(lax.optimization_barrier(jnp.sum(grad_heads * attended, axis=3)), (1, 2, 0))

    def backward(grad_query, block_items):
        raw_scores, visible_mask = scores(block_items)
        weights = weighting(raw_scores, visible_mask)
        probs_bf = weights.astype(jnp.bfloat16).astype(jnp.float32)
        key_block = block_items[0].astype(jnp.float32)
        value_block = block_items[1].astype(jnp.float32)
        prob_grad = jnp.einsum('rhgd,jhd->hgrj', grad_heads, value_block, precision=HIGHEST)
        score_grad = (weights * (prob_grad - row_delta[..., None])).astype(jnp.bfloat16).astype(jnp.float32)
        value_sum = jnp.einsum('hgrj,rhgd->jhd', probs_bf, grad_heads, precision=HIGHEST)
        key_sum = jnp.einsum('hgrj,rhgd->jhd', score_grad, query_heads, precision=HIGHEST) * score_scale
        grad_query = grad_query + jnp.einsum('hgrj,jhd->rhgd', score_grad, key_block, precision=HIGHEST)
        return (grad_query, (key_sum, value_sum))
    grad_query, (key_sums, value_sums) = lax.scan(backward, jnp.zeros(query_heads.shape, jnp.float32), stacked)
    return (grad_query * score_scale, key_sums.reshape(key_count, head_count, head_size), value_sums.reshape(key_count, head_count, head_size))

def rounded_part(values):
    narrow = lax.optimization_barrier(values.astype(jnp.bfloat16))
    return narrow.astype(jnp.float32)

def reference(query, grad_out, continuation_key, continuation_value, prompt_key, shared_prompt_value, assign, lengths, offsets):
    row_count = query.shape[0] // N_CAND
    prompt_len = prompt_key.shape[0]
    head_count = prompt_key.shape[1] // HEAD_WIDTH
    prompt_keys = prompt_key.reshape(prompt_len, head_count, HEAD_WIDTH)
    prompt_values = shared_prompt_value.reshape(prompt_len, head_count, HEAD_WIDTH)

    def per_device(state_pair, device):
        first_row = device * row_count
        queries = lax.dynamic_slice_in_dim(query, first_row, row_count, 0)
        grad_rows = lax.dynamic_slice_in_dim(grad_out, first_row, row_count, 0)
        cont_keys = lax.dynamic_slice_in_dim(continuation_key, first_row, row_count, 0).reshape(row_count, head_count, HEAD_WIDTH)
        cont_values = lax.dynamic_slice_in_dim(continuation_value, first_row, row_count, 0).reshape(row_count, head_count, HEAD_WIDTH)
        row_valid, row_segment, offset_row = slot_layout(assign, lengths, offsets, device, row_count)
        joined_keys = jnp.concatenate([prompt_keys, cont_keys], axis=0)
        joined_values = jnp.concatenate([prompt_values, cont_values], axis=0)
        key_segment = jnp.concatenate([jnp.full((prompt_len,), -1, jnp.int32), jnp.where(row_valid, row_segment, -2).astype(jnp.int32)])
        key_position = jnp.concatenate([jnp.arange(prompt_len, dtype=jnp.int32), jnp.arange(row_count, dtype=jnp.int32)])
        grad_query, key_sums, value_sums = attend(queries, grad_rows, joined_keys, joined_values, key_segment, key_position, row_valid, row_segment, offset_row)
        new_pair = (state_pair[0] + rounded_part(key_sums[:prompt_len]), state_pair[1] + rounded_part(value_sums[:prompt_len]))
        outputs = (grad_query.reshape(row_count, -1).astype(jnp.bfloat16), key_sums[prompt_len:].reshape(row_count, -1).astype(jnp.bfloat16), value_sums[prompt_len:].reshape(row_count, -1).astype(jnp.bfloat16))
        return (new_pair, outputs)
    zero_grad = jnp.zeros((prompt_len, head_count, HEAD_WIDTH), jnp.float32)
    (key_total, value_total), (query_grads, key_grads, value_grads) = lax.scan(per_device, (zero_grad, zero_grad), jnp.arange(N_CAND, dtype=jnp.int32))
    return (query_grads.reshape(query.shape[0], -1), key_grads.reshape(query.shape[0], -1), value_grads.reshape(query.shape[0], -1), key_total.reshape(prompt_len, -1).astype(jnp.bfloat16), value_total.reshape(prompt_len, -1).astype(jnp.bfloat16))
```

```python
import functools
import math

import jax
import jax.numpy as jnp
from jax import lax
from jax.experimental import pallas as pl
from jax.experimental.pallas import tpu as pltpu
from jax.sharding import PartitionSpec as P

HEAD_WIDTH = 128
MASKED_SCORE = -1e30
F32 = jnp.float32
BF16 = jnp.bfloat16
VMEM_BYTES = 48 * 1024 * 1024
DIMS_NT = (((1,), (1,)), ((), ()))
DIMS_NN = (((1,), (0,)), ((), ()))


def vmem_spec():
    return pl.BlockSpec(memory_space=pltpu.VMEM)


def smem_spec():
    return pl.BlockSpec(memory_space=pltpu.SMEM)


def glue_call(body, out_shape, operands, scalars=1, name=None):
    return pl.pallas_call(
        body,
        out_shape=out_shape,
        in_specs=[smem_spec()] * scalars + [vmem_spec()] * (len(operands) - scalars),
        out_specs=[vmem_spec()] * len(out_shape),
        compiler_params=pltpu.CompilerParams(vmem_limit_bytes=VMEM_BYTES),
        name=name,
    )(*operands)


def split_heads(where, prompt_key, prompt_value, parts, width):
    rows = prompt_key.shape[0]

    def body(where_ref, key_ref, value_ref, *out_refs):
        for step in range(parts):
            target = lax.rem(where_ref[0] + step, parts)
            columns = pl.ds(pl.multiple_of(target * width, width), width)
            out_refs[step][:, :width] = key_ref[:, columns]
            out_refs[step][:, width:] = value_ref[:, columns]

    shapes = [jax.ShapeDtypeStruct((rows, 2 * width), BF16)] * parts
    return glue_call(body, shapes, (where, prompt_key, prompt_value), name="split_heads")


def join_rows(pieces):
    rows, width = pieces[0].shape

    def body(*refs):
        out_ref = refs[-1]
        out_ref[...] = jnp.concatenate(
            [ref[...].astype(F32) for ref in refs[:-1]], axis=0
        ).astype(BF16)

    shapes = [jax.ShapeDtypeStruct((rows * len(pieces), width), BF16)]
    return glue_call(body, shapes, tuple(pieces), scalars=0, name="join_rows")[0]


def add_sibling(kept, arrived):
    chips, rows, width = kept.shape

    def body(kept_ref, arrived_ref, *out_refs):
        for step in range(chips):
            out_refs[step][...] = (
                kept_ref[step].astype(F32) + arrived_ref[step].astype(F32)
            ).astype(BF16)

    shapes = [jax.ShapeDtypeStruct((rows, width), BF16)] * chips
    return glue_call(body, shapes, (kept, arrived), scalars=0, name="add_sibling")


def add_chips(pieces, parts):
    rows, width = pieces[0].shape
    own = rows // parts

    def body(*refs):
        count = len(pieces)
        total = refs[0][...].astype(F32)
        for ref in refs[1:count]:
            total = total + ref[...].astype(F32)
        for step in range(parts):
            refs[count + step][...] = total[step * own : (step + 1) * own].astype(BF16)

    shapes = [jax.ShapeDtypeStruct((own, width), BF16)] * parts
    return glue_call(body, shapes, tuple(pieces), scalars=0, name="add_chips")


def merge_heads(where, pieces):
    rows, double = pieces[0].shape
    width = double // 2
    parts = len(pieces)

    def body(where_ref, *refs):
        key_ref, value_ref = refs[-2:]
        for step in range(parts):
            source = lax.rem(where_ref[0] + parts - step, parts)
            columns = pl.ds(pl.multiple_of(source * width, width), width)
            key_ref[:, columns] = refs[step][:, :width]
            value_ref[:, columns] = refs[step][:, width:]

    shapes = [jax.ShapeDtypeStruct((rows, width * parts), BF16)] * 2
    return glue_call(body, shapes, (where, *pieces), name="merge_heads")


def attention_body(
    prefix_count,
    cand_count,
    own_rows,
    window,
    per_device,
    heads,
    group,
    where_ref,
    assign_ref,
    lengths_ref,
    offsets_ref,
    *refs,
):
    chips = cand_count // 2
    pieces = refs[:cand_count]
    q_ref, g_ref, ck_ref, cv_ref = refs[cand_count : cand_count + 4]
    dq_ref, dck_ref, dcv_ref, keep_ref, send_ref = refs[cand_count + 4 : cand_count + 9]
    (
        table,
        stage,
        keys,
        values,
        keys_t,
        score,
        dprob,
        expo,
        sgrad,
        acc,
        cacc_k,
        cacc_v,
    ) = refs[cand_count + 9 :]
    head = pl.program_id(0)
    win = pl.program_id(1)
    windows = pl.num_programs(1)
    prompt_len = keys.shape[1]
    half = prompt_len // 2
    chunk = math.gcd(half, 128)
    band = 2 * window
    lanes = group * window
    groups = q_ref.shape[1] // HEAD_WIDTH // group
    scale = 1.0 / math.sqrt(HEAD_WIDTH)
    my_prefix = where_ref[0]
    my_cand = where_ref[1]
    width = heads * HEAD_WIDTH

    def token_base(prefix_index, cand_index):
        return pl.multiple_of((prefix_index * cand_count + cand_index) * own_rows, 8)

    @pl.when((head == 0) & (win == 0))
    def _():
        def visit(k, carry):
            count, place = carry
            mine = assign_ref[k] == my_cand

            @pl.when(mine)
            def _():
                table[0, count] = place
                table[1, count] = place + lengths_ref[k]
                table[2, count] = offsets_ref[k]

            return (
                count + mine.astype(jnp.int32),
                place + jnp.where(mine, lengths_ref[k], 0),
            )

        lax.fori_loop(
            0, assign_ref.shape[0], visit, (jnp.int32(0), jnp.int32(0))
        )
        sibling = my_cand + 1 - 2 * lax.rem(my_cand, 2)
        for side, base_cand in ((0, my_cand), (1, sibling)):
            for step in range(chips):
                source = lax.rem(base_cand + 2 * (chips - step), cand_count)
                block = pieces[side * chips + step][...].astype(F32)
                for turn in range(prefix_count):
                    origin = lax.rem(my_prefix + prefix_count - turn, prefix_count)
                    stage[pl.ds(token_base(origin, source), own_rows), :] = block[
                        turn * own_rows : (turn + 1) * own_rows
                    ]
        for h in range(heads):
            k_block = stage[:, h * HEAD_WIDTH : (h + 1) * HEAD_WIDTH]
            keys[h] = k_block.astype(BF16)
            keys_t[h] = k_block.T.astype(BF16)
            values[h] = stage[:, width + h * HEAD_WIDTH : width + (h + 1) * HEAD_WIDTH].astype(
                BF16
            )

    @pl.when(win == 0)
    def _():
        acc[...] = jnp.zeros_like(acc)
        cacc_k[...] = jnp.zeros_like(cacc_k)
        cacc_v[...] = jnp.zeros_like(cacc_v)

    first_row = win * window
    filled = table[1, per_device - 1]

    @pl.when(first_row >= filled)
    def _():
        dq_ref[...] = jnp.zeros_like(dq_ref)

    @pl.when(first_row < filled)
    def _():
        band_row = pl.multiple_of(jnp.maximum(first_row - window, 0), window)
        row = first_row + lax.broadcasted_iota(jnp.int32, (1, lanes), 1) % window
        offset = jnp.zeros((1, lanes), jnp.int32)
        start = jnp.full((1, lanes), windows * window, jnp.int32)
        for c in range(per_device):
            inside = (row >= table[0, c]) & (row < table[1, c])
            offset = jnp.where(inside, table[2, c], offset)
            start = jnp.where(inside, table[0, c], start)
        valid = row < filled
        blocks = [(i * chunk, chunk) for i in range(prompt_len // chunk)]

        def masked(s, first):
            if first < half:
                return s
            place = first + lax.broadcasted_iota(jnp.int32, s.shape, 0)
            return jnp.where(place < offset, s, MASKED_SCORE)

        cont_place = band_row + lax.broadcasted_iota(jnp.int32, (band, lanes), 0)
        cont_seen = (cont_place >= start) & (cont_place <= row)
        ck = ck_ref[pl.ds(band_row, band), :]
        cv = cv_ref[pl.ds(band_row, band), :]

        def fold(x, op):
            return op(x.reshape(x.shape[0] // 8, 8, x.shape[1]), axis=0)

        def rows_of(ref, index):
            return jnp.concatenate(
                [
                    ref[:, (index * group + h) * HEAD_WIDTH : (index * group + h + 1) * HEAD_WIDTH]
                    for h in range(group)
                ],
                axis=0,
            )

        factor = scale * math.log2(math.e)
        scaled_q, scaled_g = [], []
        for index in range(groups):
            q = rows_of(q_ref, index)
            g = rows_of(g_ref, index)
            cols = slice(index * lanes, (index + 1) * lanes)
            top = jnp.full((8, lanes), MASKED_SCORE, F32)
            for first, size in blocks:
                s = lax.dot_general(
                    keys[head, first : first + size], q, DIMS_NT, preferred_element_type=F32
                )
                s = masked(s * factor, first)
                score[first : first + size, cols] = s
                top = jnp.maximum(top, fold(s, jnp.max))
            s = lax.dot_general(ck, q, DIMS_NT, preferred_element_type=F32)
            s = jnp.where(cont_seen, s * factor, MASKED_SCORE)
            score[prompt_len:, cols] = s
            top = jnp.maximum(top, fold(s, jnp.max))
            top = jnp.max(top, axis=0, keepdims=True)
            total = jnp.zeros((8, lanes), F32)
            delta = jnp.zeros((8, lanes), F32)
            for first, size in blocks + [(prompt_len, band)]:
                v = values[head, first : first + size] if first < prompt_len else cv
                dp = lax.dot_general(v, g, DIMS_NT, preferred_element_type=F32)
                e = jnp.exp2(score[first : first + size, cols] - top)
                dprob[first : first + size, cols] = dp
                expo[first : first + size, cols] = e.astype(BF16)
                total = total + fold(e, jnp.sum)
                delta = delta + fold(e * dp, jnp.sum)
            total = jnp.sum(total, axis=0, keepdims=True)
            delta = jnp.sum(delta, axis=0, keepdims=True)
            inverse = jnp.where(valid, 1.0 / total, 0.0)
            delta = delta / total
            for first, size in blocks + [(prompt_len, band)]:
                e = expo[first : first + size, cols].astype(F32)
                sgrad[first : first + size, cols] = (
                    e * (dprob[first : first + size, cols] - delta)
                ).astype(BF16)
            column = jnp.broadcast_to(inverse, (HEAD_WIDTH, lanes)).T
            scaled_q.append((q.astype(F32) * (column * scale)).astype(BF16))
            scaled_g.append((g.astype(F32) * column).astype(BF16))
            dq_t = lax.dot_general(
                keys_t[head], sgrad[:prompt_len, cols], DIMS_NN, preferred_element_type=F32
            ) + lax.dot_general(
                ck.astype(F32).T.astype(BF16),
                sgrad[prompt_len:, cols],
                DIMS_NN,
                preferred_element_type=F32,
            )
            dq = (dq_t * (inverse * scale)).T.astype(BF16)
            for h in range(group):
                place = (index * group + h) * HEAD_WIDTH
                dq_ref[:, place : place + HEAD_WIDTH] = dq[h * window : (h + 1) * window]
        q_all = jnp.concatenate(scaled_q, axis=0)
        g_all = jnp.concatenate(scaled_g, axis=0)
        acc[:, :HEAD_WIDTH] += lax.dot_general(
            sgrad[:prompt_len, :], q_all, DIMS_NN, preferred_element_type=F32
        )
        acc[:, HEAD_WIDTH:] += lax.dot_general(
            expo[:prompt_len, :], g_all, DIMS_NN, preferred_element_type=F32
        )
        cacc_k[pl.ds(band_row, band), :] += lax.dot_general(
            sgrad[prompt_len:, :], q_all, DIMS_NN, preferred_element_type=F32
        )
        cacc_v[pl.ds(band_row, band), :] += lax.dot_general(
            expo[prompt_len:, :], g_all, DIMS_NN, preferred_element_type=F32
        )

    @pl.when(win == windows - 1)
    def _():
        dck_ref[...] = cacc_k[...].astype(BF16)
        dcv_ref[...] = cacc_v[...].astype(BF16)
        sibling = my_cand + 1 - 2 * lax.rem(my_cand, 2)
        for out_ref, base_cand in ((keep_ref, my_cand), (send_ref, sibling)):
            for step in range(chips):
                target = lax.rem(base_cand + 2 * step, cand_count)
                block = jnp.concatenate(
                    [
                        acc[
                            pl.ds(
                                token_base(lax.rem(my_prefix + turn, prefix_count), target),
                                own_rows,
                            ),
                            :,
                        ]
                        for turn in range(prefix_count)
                    ],
                    axis=0,
                ).astype(BF16)
                for h in range(heads):

                    @pl.when(head == h)
                    def _(block=block, h=h, step=step, out_ref=out_ref):
                        out_ref[step, :, h * HEAD_WIDTH : (h + 1) * HEAD_WIDTH] = block[
                            :, :HEAD_WIDTH
                        ]
                        out_ref[
                            step, :, width + h * HEAD_WIDTH : width + (h + 1) * HEAD_WIDTH
                        ] = block[:, HEAD_WIDTH:]


def attention(
    where, assign, lengths, offsets, pieces, query, grad_out, cont_key, cont_value, axes
):
    prefix_count, cand_count = axes
    rows, query_width = query.shape
    heads = cont_key.shape[1] // HEAD_WIDTH
    head_columns = query_width // heads
    per_device = assign.shape[0] // cand_count
    window = rows // per_device
    piece_rows, piece_width = pieces[0].shape
    own_rows = piece_rows // prefix_count
    prompt_len = piece_rows * cand_count
    group = min(max(256 // window, 1), head_columns // HEAD_WIDTH)
    all_lanes = head_columns // HEAD_WIDTH * window
    joined = prompt_len + 2 * window
    chips = cand_count // 2
    by_window = pl.BlockSpec((window, head_columns), lambda h, w, *_: (w, h))
    by_head = pl.BlockSpec((rows, HEAD_WIDTH), lambda h, w, *_: (0, h))
    whole_piece = pl.BlockSpec((piece_rows, piece_width), lambda h, w, *_: (0, 0))
    parts_spec = pl.BlockSpec((chips, piece_rows, piece_width), lambda h, w, *_: (0, 0, 0))
    flops = 10 * query.size * joined
    return pl.pallas_call(
        functools.partial(
            attention_body,
            prefix_count,
            cand_count,
            own_rows,
            window,
            per_device,
            heads,
            group,
        ),
        grid_spec=pltpu.PrefetchScalarGridSpec(
            num_scalar_prefetch=4,
            grid=(heads, per_device),
            in_specs=[whole_piece] * cand_count + [by_window, by_window, by_head, by_head],
            out_specs=[by_window, by_head, by_head, parts_spec, parts_spec],
            scratch_shapes=[
                pltpu.SMEM((3, per_device), jnp.int32),
                pltpu.VMEM((prompt_len, piece_width), F32),
                pltpu.VMEM((heads, prompt_len, HEAD_WIDTH), BF16),
                pltpu.VMEM((heads, prompt_len, HEAD_WIDTH), BF16),
                pltpu.VMEM((heads, HEAD_WIDTH, prompt_len), BF16),
                pltpu.VMEM((joined, all_lanes), F32),
                pltpu.VMEM((joined, all_lanes), F32),
                pltpu.VMEM((joined, all_lanes), BF16),
                pltpu.VMEM((joined, all_lanes), BF16),
                pltpu.VMEM((prompt_len, 2 * HEAD_WIDTH), F32),
                pltpu.VMEM((rows, HEAD_WIDTH), F32),
                pltpu.VMEM((rows, HEAD_WIDTH), F32),
            ],
        ),
        out_shape=[
            jax.ShapeDtypeStruct(query.shape, BF16),
            jax.ShapeDtypeStruct(cont_key.shape, BF16),
            jax.ShapeDtypeStruct(cont_value.shape, BF16),
            jax.ShapeDtypeStruct((chips, piece_rows, piece_width), BF16),
            jax.ShapeDtypeStruct((chips, piece_rows, piece_width), BF16),
        ],
        compiler_params=pltpu.CompilerParams(
            dimension_semantics=("arbitrary", "arbitrary"), vmem_limit_bytes=VMEM_BYTES
        ),
        cost_estimate=pl.CostEstimate(
            flops=flops, bytes_accessed=8 * query.size, transcendentals=query.size * 4
        ),
        name="attention_backward",
    )(where, assign, lengths, offsets, *pieces, query, grad_out, cont_key, cont_value)


def per_device(
    query,
    grad_out,
    continuation_key,
    continuation_value,
    prompt_key,
    shared_prompt_value,
    assign,
    lengths,
    offsets,
):
    prefix_count = lax.axis_size("prefix")
    cand_count = lax.axis_size("cand")
    chips = cand_count // 2
    where = jnp.stack([lax.axis_index("prefix"), lax.axis_index("cand")]).astype(jnp.int32)
    local_width = prompt_key.shape[1] // prefix_count

    def along_prefix(x, step):
        return lax.ppermute(
            x, "prefix", [(i, (i + step) % prefix_count) for i in range(prefix_count)]
        )

    def along_chips(x, step):
        return lax.ppermute(
            x, "cand", [(i, (i + 2 * step) % cand_count) for i in range(cand_count)]
        )

    def to_sibling(x):
        return lax.ppermute(x, "cand", [(i, i ^ 1) for i in range(cand_count)])

    split = split_heads(where, prompt_key, shared_prompt_value, prefix_count, local_width)
    held = join_rows([split[0]] + [along_prefix(split[d], d) for d in range(1, prefix_count)])
    same_core = [held] + [along_chips(held, d) for d in range(1, chips)]
    other_core = [to_sibling(x) for x in same_core]
    query_grad, cont_key_grad, cont_value_grad, kept, sent = attention(
        where,
        assign,
        lengths,
        offsets,
        same_core + other_core,
        query,
        grad_out,
        continuation_key,
        continuation_value,
        (prefix_count, cand_count),
    )
    by_chip = add_sibling(kept, to_sibling(sent))
    split_sums = add_chips(
        [by_chip[0]] + [along_chips(by_chip[d], d) for d in range(1, chips)], prefix_count
    )
    prompt_key_grad, prompt_value_grad = merge_heads(
        where, [split_sums[0]] + [along_prefix(split_sums[d], d) for d in range(1, prefix_count)]
    )
    return (query_grad, cont_key_grad, cont_value_grad, prompt_key_grad, prompt_value_grad)


def solution(mesh):
    in_specs = (
        P("cand", "prefix"),
        P("cand", "prefix"),
        P("cand", "prefix"),
        P("cand", "prefix"),
        P(("prefix", "cand"), None),
        P(("prefix", "cand"), None),
        P(),
        P(),
        P(),
    )
    out_specs = (
        P("cand", "prefix"),
        P("cand", "prefix"),
        P("cand", "prefix"),
        P(("prefix", "cand"), None),
        P(("prefix", "cand"), None),
    )
    return jax.shard_map(
        per_device, mesh=mesh, in_specs=in_specs, out_specs=out_specs, check_vma=False
    )
```

```python
import functools
import math

import jax
import jax.numpy as jnp
from jax import lax
from jax.experimental import pallas as pl
from jax.experimental.pallas import tpu as pltpu
from jax.sharding import PartitionSpec as P

HEAD_WIDTH = 128
MASKED_SCORE = -1e30
F32 = jnp.float32
BF16 = jnp.bfloat16
VMEM_BYTES = 40 * 1024 * 1024
GLUE_VMEM_BYTES = 8 * 1024 * 1024
DIMS_NT = (((1,), (1,)), ((), ()))
DIMS_NN = (((1,), (0,)), ((), ()))


def vmem_spec():
    return pl.BlockSpec(memory_space=pltpu.VMEM)


def smem_spec():
    return pl.BlockSpec(memory_space=pltpu.SMEM)


def glue_call(body, out_shape, operands, scalars=1, name=None):
    return pl.pallas_call(
        body,
        out_shape=out_shape,
        in_specs=[smem_spec()] * scalars + [vmem_spec()] * (len(operands) - scalars),
        out_specs=[vmem_spec()] * len(out_shape),
        compiler_params=pltpu.CompilerParams(vmem_limit_bytes=GLUE_VMEM_BYTES),
        name=name,
    )(*operands)


def split_heads(prompt_key, prompt_value, parts, chips):
    rows, full = prompt_key.shape
    width = full // parts

    def body(key_hbm, value_hbm, out_ref, key_ref, value_ref, sems):
        copies = [
            pltpu.make_async_copy(key_hbm, key_ref, sems.at[0]),
            pltpu.make_async_copy(value_hbm, value_ref, sems.at[1]),
        ]
        for copy in copies:
            copy.start()
        for copy in copies:
            copy.wait()
        for q in range(parts):
            for z in range(chips):
                out_ref[q * chips + z, :, :width] = key_ref[:, q * width : (q + 1) * width]
                out_ref[q * chips + z, :, width:] = value_ref[:, q * width : (q + 1) * width]

    return pl.pallas_call(
        body,
        out_shape=jax.ShapeDtypeStruct((parts * chips, rows, 2 * width), BF16),
        in_specs=[pl.BlockSpec(memory_space=pl.ANY)] * 2,
        out_specs=vmem_spec(),
        scratch_shapes=[
            pltpu.VMEM(prompt_key.shape, BF16),
            pltpu.VMEM(prompt_value.shape, BF16),
            pltpu.SemaphoreType.DMA((2,)),
        ],
        compiler_params=pltpu.CompilerParams(vmem_limit_bytes=GLUE_VMEM_BYTES),
        name="split_heads",
    )(prompt_key, prompt_value)


def add_sibling(kept, arrived):
    def body(kept_ref, arrived_ref, out_ref):
        for i in range(kept.shape[0]):
            out_ref[i] = (kept_ref[i].astype(F32) + arrived_ref[i].astype(F32)).astype(BF16)

    shapes = [jax.ShapeDtypeStruct(kept.shape, BF16)]
    return glue_call(body, shapes, (kept, arrived), scalars=0, name="add_sibling")[0]


def add_chips(pieces, parts, chips):
    rows, double = pieces.shape[1:]
    width = double // 2

    def body(piece_ref, key_ref, value_ref):
        for p in range(parts):
            total = piece_ref[p * chips].astype(F32)
            for z in range(1, chips):
                total = total + piece_ref[p * chips + z].astype(F32)
            total = total.astype(BF16)
            key_ref[:, p * width : (p + 1) * width] = total[:, :width]
            value_ref[:, p * width : (p + 1) * width] = total[:, width:]

    shapes = [jax.ShapeDtypeStruct((rows, width * parts), BF16)] * 2
    return glue_call(body, shapes, (pieces,), scalars=0, name="add_chips")


def attention_body(
    prefix_count,
    cand_count,
    window,
    per_device,
    heads,
    group,
    where_ref,
    assign_ref,
    lengths_ref,
    offsets_ref,
    own_ref,
    other_ref,
    ck_ref,
    cv_ref,
    q_hbm,
    g_hbm,
    dq_hbm,
    dck_ref,
    dcv_ref,
    keep_ref,
    send_ref,
    table,
    stage,
    keys,
    values,
    keys_t,
    q_ref,
    g_ref,
    dq_ref,
    score,
    dprob,
    expo,
    sgrad,
    acc,
    cacc_k,
    cacc_v,
    in_sems,
    out_sems,
):
    chips = cand_count // 2
    own_rows = own_ref.shape[1]
    windows = per_device
    steps = heads * windows
    prompt_len = keys.shape[1]
    half = prompt_len // 2
    levels = 3 if half % (3 * 128) == 0 else 1
    chunk = math.gcd(half, 128)
    band = 2 * window
    lanes = group * window
    head_columns = q_ref.shape[2]
    groups = head_columns // HEAD_WIDTH // group
    scale = 1.0 / math.sqrt(HEAD_WIDTH)
    factor = scale * math.log2(math.e)
    width = heads * HEAD_WIDTH
    my_cand = where_ref[0]
    my_core = lax.rem(my_cand, 2)

    def copy_in(t, which):
        src, dst = ((q_hbm, q_ref), (g_hbm, g_ref))[which]
        h, w = divmod(t, windows)
        return pltpu.make_async_copy(
            src.at[w * window : (w + 1) * window, h * head_columns : (h + 1) * head_columns],
            dst.at[t],
            in_sems.at[which, t],
        )

    def copy_out(t):
        h, w = divmod(t, windows)
        return pltpu.make_async_copy(
            dq_ref.at[t],
            dq_hbm.at[w * window : (w + 1) * window, h * head_columns : (h + 1) * head_columns],
            out_sems.at[t],
        )

    for t in range(steps):
        copy_in(t, 0).start()
        copy_in(t, 1).start()

    def visit(k, carry):
        count, place = carry
        mine = assign_ref[k] == my_cand

        @pl.when(mine)
        def _():
            table[0, count] = place
            table[1, count] = place + lengths_ref[k]
            table[2, count] = offsets_ref[k]

        return (
            count + mine.astype(jnp.int32),
            place + jnp.where(mine, lengths_ref[k], 0),
        )

    lax.fori_loop(0, assign_ref.shape[0], visit, (jnp.int32(0), jnp.int32(0)))
    filled = table[1, per_device - 1]

    def token_base(q, z, core):
        return pl.multiple_of((q * cand_count + 2 * z + core) * own_rows, 8)

    for ref, core in ((own_ref, my_core), (other_ref, 1 - my_core)):
        for q in range(prefix_count):
            for z in range(chips):
                stage[pl.ds(token_base(q, z, core), own_rows), :] = ref[q * chips + z].astype(F32)
    for h in range(heads):
        k_block = stage[:, h * HEAD_WIDTH : (h + 1) * HEAD_WIDTH]
        keys[h] = k_block.astype(BF16)
        keys_t[h] = k_block.T.astype(BF16)
        values[h] = stage[:, width + h * HEAD_WIDTH : width + (h + 1) * HEAD_WIDTH].astype(BF16)
    acc[...] = jnp.zeros_like(acc)
    cacc_k[...] = jnp.zeros_like(cacc_k)
    cacc_v[...] = jnp.zeros_like(cacc_v)

    def fold(x, op):
        return op(x.reshape(x.shape[0] // 8, 8, x.shape[1]), axis=0)

    def attend(t, prompt_rows):
        head = t // windows
        first_row = lax.rem(t, windows) * window
        band_row = pl.multiple_of(jnp.maximum(first_row - window, 0), window)
        row = first_row + lax.broadcasted_iota(jnp.int32, (1, lanes), 1) % window
        offset = jnp.zeros((1, lanes), jnp.int32)
        start = jnp.full((1, lanes), windows * window, jnp.int32)
        for c in range(per_device):
            inside = (row >= table[0, c]) & (row < table[1, c])
            offset = jnp.where(inside, table[2, c], offset)
            start = jnp.where(inside, table[0, c], start)
        valid = row < filled
        blocks = [(i * chunk, chunk) for i in range(prompt_rows // chunk)]
        every = blocks + [(prompt_len, band)]
        cont_place = band_row + lax.broadcasted_iota(jnp.int32, (band, lanes), 0)
        cont_seen = (cont_place >= start) & (cont_place <= row)
        ck = ck_ref[head, pl.ds(band_row, band), :]
        cv = cv_ref[head, pl.ds(band_row, band), :]

        def rows_of(ref, index):
            return jnp.concatenate(
                [
                    ref[t, :, (index * group + h) * HEAD_WIDTH : (index * group + h + 1) * HEAD_WIDTH]
                    for h in range(group)
                ],
                axis=0,
            )

        qs = [rows_of(q_ref, i) for i in range(groups)]
        gs = [rows_of(g_ref, i) for i in range(groups)]
        cols = [slice(i * lanes, (i + 1) * lanes) for i in range(groups)]
        tops = []
        for i in range(groups):
            top = jnp.full((8, lanes), MASKED_SCORE, F32)
            for first, size in every:
                k = keys[head, first : first + size] if first < prompt_len else ck
                s = lax.dot_general(k, qs[i], DIMS_NT, preferred_element_type=F32) * factor
                if first == prompt_len:
                    s = jnp.where(cont_seen, s, MASKED_SCORE)
                elif first >= half:
                    place = first + lax.broadcasted_iota(jnp.int32, s.shape, 0)
                    s = jnp.where(place < offset, s, MASKED_SCORE)
                score[first : first + size, cols[i]] = s
                top = jnp.maximum(top, fold(s, jnp.max))
            tops.append(jnp.max(top, axis=0, keepdims=True))
        totals, deltas = [], []
        for i in range(groups):
            total = jnp.zeros((8, lanes), F32)
            delta = jnp.zeros((8, lanes), F32)
            for first, size in every:
                v = values[head, first : first + size] if first < prompt_len else cv
                dp = lax.dot_general(v, gs[i], DIMS_NT, preferred_element_type=F32)
                e = jnp.exp2(score[first : first + size, cols[i]] - tops[i])
                dprob[first : first + size, cols[i]] = dp
                expo[first : first + size, cols[i]] = e.astype(BF16)
                total = total + fold(e, jnp.sum)
                delta = delta + fold(e * dp, jnp.sum)
            totals.append(jnp.sum(total, axis=0, keepdims=True))
            deltas.append(jnp.sum(delta, axis=0, keepdims=True))
        inverses, scaled_q, scaled_g = [], [], []
        for i in range(groups):
            inverse = jnp.where(valid, 1.0 / totals[i], 0.0)
            delta = deltas[i] / totals[i]
            for first, size in every:
                e = expo[first : first + size, cols[i]].astype(F32)
                sgrad[first : first + size, cols[i]] = (
                    e * (dprob[first : first + size, cols[i]] - delta)
                ).astype(BF16)
            column = jnp.broadcast_to(inverse, (HEAD_WIDTH, lanes)).T
            scaled_q.append((qs[i].astype(F32) * (column * scale)).astype(BF16))
            scaled_g.append((gs[i].astype(F32) * column).astype(BF16))
            inverses.append(inverse)
        g_all = jnp.concatenate(scaled_g, axis=0)
        q_all = jnp.concatenate(scaled_q, axis=0)
        acc[head, :prompt_rows, HEAD_WIDTH:] += lax.dot_general(
            expo[:prompt_rows, :], g_all, DIMS_NN, preferred_element_type=F32
        )
        cacc_v[head, pl.ds(band_row, band), :] += lax.dot_general(
            expo[prompt_len:, :], g_all, DIMS_NN, preferred_element_type=F32
        )
        acc[head, :prompt_rows, :HEAD_WIDTH] += lax.dot_general(
            sgrad[:prompt_rows, :], q_all, DIMS_NN, preferred_element_type=F32
        )
        cacc_k[head, pl.ds(band_row, band), :] += lax.dot_general(
            sgrad[prompt_len:, :], q_all, DIMS_NN, preferred_element_type=F32
        )
        ck_t = ck.astype(F32).T.astype(BF16)
        for i in range(groups):
            dq_t = lax.dot_general(
                keys_t[head, :, :prompt_rows],
                sgrad[:prompt_rows, cols[i]],
                DIMS_NN,
                preferred_element_type=F32,
            ) + lax.dot_general(
                ck_t, sgrad[prompt_len:, cols[i]], DIMS_NN, preferred_element_type=F32
            )
            dq = (dq_t * (inverses[i] * scale)).T.astype(BF16)
            for h in range(group):
                place = (i * group + h) * HEAD_WIDTH
                dq_ref[t, :, place : place + HEAD_WIDTH] = dq[h * window : (h + 1) * window]

    for t in range(steps):
        copy_in(t, 0).wait()
        copy_in(t, 1).wait()

    def step(t, carry):
        first_row = lax.rem(t, windows) * window
        reach = jnp.int32(0)
        for c in range(per_device):
            meets = (table[0, c] < first_row + window) & (table[1, c] > first_row)
            reach = jnp.maximum(reach, jnp.where(meets, table[2, c], 0))
        grain = half // levels
        level = jnp.where(
            first_row >= filled, levels + 1, (jnp.maximum(reach - half, 0) + grain - 1) // grain
        )
        for n in range(levels + 1):

            @pl.when(level == n)
            def _(n=n):
                attend(t, half + n * grain)

        @pl.when(level == levels + 1)
        def _():
            dq_ref[t] = jnp.zeros(dq_ref.shape[1:], BF16)

        return carry

    lax.fori_loop(0, steps, step, jnp.int32(0))
    for t in range(steps):
        copy_out(t).start()
    for h in range(heads):
        here = slice(h * HEAD_WIDTH, (h + 1) * HEAD_WIDTH)
        dck_ref[:, here] = cacc_k[h].astype(BF16)
        dcv_ref[:, here] = cacc_v[h].astype(BF16)
    for ref, core in ((keep_ref, my_core), (send_ref, 1 - my_core)):
        for q in range(prefix_count):
            for z in range(chips):
                for h in range(heads):
                    block = acc[h, pl.ds(token_base(q, z, core), own_rows), :].astype(BF16)
                    here = slice(h * HEAD_WIDTH, (h + 1) * HEAD_WIDTH)
                    ref[q * chips + z, :, here] = block[:, :HEAD_WIDTH]
                    there = slice(width + h * HEAD_WIDTH, width + (h + 1) * HEAD_WIDTH)
                    ref[q * chips + z, :, there] = block[:, HEAD_WIDTH:]
    for t in range(steps):
        copy_out(t).wait()


def attention(
    where, assign, lengths, offsets, own, other, query, grad_out, cont_key, cont_value, axes
):
    prefix_count, cand_count = axes
    rows, query_width = query.shape
    heads = cont_key.shape[1] // HEAD_WIDTH
    head_columns = query_width // heads
    per_device = assign.shape[0] // cand_count
    window = rows // per_device
    piece_width = own.shape[2]
    prompt_len = 2 * own.shape[0] * own.shape[1]
    group = min(max(256 // window, 1), head_columns // HEAD_WIDTH)
    all_lanes = head_columns // HEAD_WIDTH * window
    joined = prompt_len + 2 * window
    steps = heads * per_device
    in_hbm = pl.BlockSpec(memory_space=pl.ANY)

    def by_head(x):
        return jnp.stack([x[:, h * HEAD_WIDTH : (h + 1) * HEAD_WIDTH] for h in range(heads)])

    return pl.pallas_call(
        functools.partial(
            attention_body, prefix_count, cand_count, window, per_device, heads, group
        ),
        in_specs=[smem_spec()] * 4 + [vmem_spec()] * 4 + [in_hbm] * 2,
        out_specs=[in_hbm] + [vmem_spec()] * 4,
        scratch_shapes=[
            pltpu.SMEM((3, per_device), jnp.int32),
            pltpu.VMEM((prompt_len, piece_width), F32),
            pltpu.VMEM((heads, prompt_len, HEAD_WIDTH), BF16),
            pltpu.VMEM((heads, prompt_len, HEAD_WIDTH), BF16),
            pltpu.VMEM((heads, HEAD_WIDTH, prompt_len), BF16),
            pltpu.VMEM((steps, window, head_columns), BF16),
            pltpu.VMEM((steps, window, head_columns), BF16),
            pltpu.VMEM((steps, window, head_columns), BF16),
            pltpu.VMEM((joined, all_lanes), F32),
            pltpu.VMEM((joined, all_lanes), F32),
            pltpu.VMEM((joined, all_lanes), BF16),
            pltpu.VMEM((joined, all_lanes), BF16),
            pltpu.VMEM((heads, prompt_len, 2 * HEAD_WIDTH), F32),
            pltpu.VMEM((heads, rows, HEAD_WIDTH), F32),
            pltpu.VMEM((heads, rows, HEAD_WIDTH), F32),
            pltpu.SemaphoreType.DMA((2, steps)),
            pltpu.SemaphoreType.DMA((steps,)),
        ],
        out_shape=[
            jax.ShapeDtypeStruct(query.shape, BF16),
            jax.ShapeDtypeStruct(cont_key.shape, BF16),
            jax.ShapeDtypeStruct(cont_value.shape, BF16),
            jax.ShapeDtypeStruct(own.shape, BF16),
            jax.ShapeDtypeStruct(own.shape, BF16),
        ],
        compiler_params=pltpu.CompilerParams(vmem_limit_bytes=VMEM_BYTES),
        cost_estimate=pl.CostEstimate(
            flops=10 * query.size * joined,
            bytes_accessed=8 * query.size,
            transcendentals=query.size * 4,
        ),
        name="attention_backward",
    )(
        where,
        assign,
        lengths,
        offsets,
        own,
        other,
        by_head(cont_key),
        by_head(cont_value),
        query,
        grad_out,
    )


def per_device(
    query,
    grad_out,
    continuation_key,
    continuation_value,
    prompt_key,
    shared_prompt_value,
    assign,
    lengths,
    offsets,
):
    prefix_count = lax.axis_size("prefix")
    cand_count = lax.axis_size("cand")
    chips = cand_count // 2
    where = jnp.reshape(lax.axis_index("cand"), (1,)).astype(jnp.int32)
    same_core = [
        [p * cand_count + 2 * z + core for p in range(prefix_count) for z in range(chips)]
        for core in range(2)
    ]

    def exchange(x):
        return lax.all_to_all(
            x, ("prefix", "cand"), 0, 0, tiled=True, axis_index_groups=same_core
        )

    def to_sibling(x):
        return lax.ppermute(x, "cand", [(i, i ^ 1) for i in range(cand_count)])

    own = exchange(split_heads(prompt_key, shared_prompt_value, prefix_count, chips))
    query_grad, cont_key_grad, cont_value_grad, kept, sent = attention(
        where,
        assign,
        lengths,
        offsets,
        own,
        to_sibling(own),
        query,
        grad_out,
        continuation_key,
        continuation_value,
        (prefix_count, cand_count),
    )
    by_chip = exchange(add_sibling(kept, to_sibling(sent)))
    prompt_key_grad, prompt_value_grad = add_chips(by_chip, prefix_count, chips)
    return (query_grad, cont_key_grad, cont_value_grad, prompt_key_grad, prompt_value_grad)


def solution(mesh):
    in_specs = (
        P("cand", "prefix"),
        P("cand", "prefix"),
        P("cand", "prefix"),
        P("cand", "prefix"),
        P(("prefix", "cand"), None),
        P(("prefix", "cand"), None),
        P(),
        P(),
        P(),
    )
    out_specs = (
        P("cand", "prefix"),
        P("cand", "prefix"),
        P("cand", "prefix"),
        P(("prefix", "cand"), None),
        P(("prefix", "cand"), None),
    )
    return jax.shard_map(
        per_device, mesh=mesh, in_specs=in_specs, out_specs=out_specs, check_vma=False
    )
```

```python
import functools
import math

import jax
import jax.numpy as jnp
from jax import lax
from jax.experimental import pallas as pl
from jax.experimental.pallas import tpu as pltpu
from jax.sharding import PartitionSpec as P

HEAD_WIDTH = 128
MASKED_SCORE = -1e30
F32 = jnp.float32
BF16 = jnp.bfloat16
VMEM_BYTES = 40 * 1024 * 1024
GLUE_VMEM_BYTES = 8 * 1024 * 1024
DIMS_NT = (((1,), (1,)), ((), ()))
DIMS_NN = (((1,), (0,)), ((), ()))


def vmem_spec():
    return pl.BlockSpec(memory_space=pltpu.VMEM)


def smem_spec():
    return pl.BlockSpec(memory_space=pltpu.SMEM)


def glue_call(body, out_shape, operands, scalars=1, name=None):
    return pl.pallas_call(
        body,
        out_shape=out_shape,
        in_specs=[smem_spec()] * scalars + [vmem_spec()] * (len(operands) - scalars),
        out_specs=[vmem_spec()] * len(out_shape),
        compiler_params=pltpu.CompilerParams(vmem_limit_bytes=GLUE_VMEM_BYTES),
        name=name,
    )(*operands)


def split_heads(prompt_key, prompt_value, parts, chips):
    rows, full = prompt_key.shape
    width = full // parts

    def body(key_hbm, value_hbm, out_ref, key_ref, value_ref, sems):
        copies = [
            pltpu.make_async_copy(key_hbm, key_ref, sems.at[0]),
            pltpu.make_async_copy(value_hbm, value_ref, sems.at[1]),
        ]
        for copy in copies:
            copy.start()
        for copy in copies:
            copy.wait()
        for q in range(parts):
            for z in range(chips):
                out_ref[q * chips + z, :, :width] = key_ref[:, q * width : (q + 1) * width]
                out_ref[q * chips + z, :, width:] = value_ref[:, q * width : (q + 1) * width]

    return pl.pallas_call(
        body,
        out_shape=jax.ShapeDtypeStruct((parts * chips, rows, 2 * width), BF16),
        in_specs=[pl.BlockSpec(memory_space=pltpu.HBM)] * 2,
        out_specs=vmem_spec(),
        scratch_shapes=[
            pltpu.VMEM(prompt_key.shape, BF16),
            pltpu.VMEM(prompt_value.shape, BF16),
            pltpu.SemaphoreType.DMA((2,)),
        ],
        compiler_params=pltpu.CompilerParams(vmem_limit_bytes=GLUE_VMEM_BYTES),
        name="split_heads",
    )(prompt_key, prompt_value)


def add_sibling(kept, arrived):
    def body(kept_ref, arrived_ref, out_ref):
        for i in range(kept.shape[0]):
            out_ref[i] = (kept_ref[i].astype(F32) + arrived_ref[i].astype(F32)).astype(BF16)

    shapes = [jax.ShapeDtypeStruct(kept.shape, BF16)]
    return glue_call(body, shapes, (kept, arrived), scalars=0, name="add_sibling")[0]


def add_chips(pieces, parts, chips):
    rows, double = pieces.shape[1:]
    width = double // 2

    def body(piece_ref, key_ref, value_ref):
        for p in range(parts):
            total = piece_ref[p * chips].astype(F32)
            for z in range(1, chips):
                total = total + piece_ref[p * chips + z].astype(F32)
            total = total.astype(BF16)
            key_ref[:, p * width : (p + 1) * width] = total[:, :width]
            value_ref[:, p * width : (p + 1) * width] = total[:, width:]

    shapes = [jax.ShapeDtypeStruct((rows, width * parts), BF16)] * 2
    return glue_call(body, shapes, (pieces,), scalars=0, name="add_chips")


def attention_body(
    prefix_count,
    cand_count,
    window,
    per_device,
    heads,
    group,
    where_ref,
    assign_ref,
    lengths_ref,
    offsets_ref,
    own_ref,
    other_ref,
    ck_ref,
    cv_ref,
    q_ref,
    g_ref,
    dq_hbm,
    dck_ref,
    dcv_ref,
    keep_ref,
    send_ref,
    table,
    stage,
    keys,
    values,
    keys_t,
    dq_ref,
    score,
    dprob,
    expo,
    sgrad,
    acc,
    cacc_k,
    cacc_v,
    out_sems,
):
    chips = cand_count // 2
    own_rows = own_ref.shape[1]
    windows = per_device
    prompt_len = keys.shape[1]
    half = prompt_len // 2
    levels = 3 if half % (3 * 128) == 0 else 1
    grain = half // levels
    chunk = math.gcd(half, 128)
    band = 2 * window
    lanes = group * window
    head_columns = q_ref.shape[1] // heads
    per_head = head_columns // HEAD_WIDTH // group
    scale = 1.0 / math.sqrt(HEAD_WIDTH)
    factor = scale * math.log2(math.e)
    width = heads * HEAD_WIDTH
    my_cand = where_ref[0]
    my_core = lax.rem(my_cand, 2)

    count, place = jnp.int32(0), jnp.int32(0)
    for k in range(assign_ref.shape[0]):
        length = lengths_ref[k]
        table[0, count] = place
        table[1, count] = place + length
        table[2, count] = offsets_ref[k]
        mine = (assign_ref[k] == my_cand).astype(jnp.int32)
        count = count + mine
        place = place + mine * length
    filled = place

    def token_base(q, z, core):
        return pl.multiple_of((q * cand_count + 2 * z + core) * own_rows, 8)

    for ref, core in ((own_ref, my_core), (other_ref, 1 - my_core)):
        for q in range(prefix_count):
            for z in range(chips):
                stage[pl.ds(token_base(q, z, core), own_rows), :] = ref[q * chips + z].astype(F32)
    for h in range(heads):
        k_block = stage[:, h * HEAD_WIDTH : (h + 1) * HEAD_WIDTH]
        keys[h] = k_block.astype(BF16)
        keys_t[h] = k_block.T.astype(BF16)
        values[h] = stage[:, width + h * HEAD_WIDTH : width + (h + 1) * HEAD_WIDTH].astype(BF16)
    acc[...] = jnp.zeros_like(acc)
    cacc_k[...] = jnp.zeros_like(cacc_k)
    cacc_v[...] = jnp.zeros_like(cacc_v)

    def fold(x, op):
        return op(x.reshape(x.shape[0] // 8, 8, x.shape[1]), axis=0)

    def copy_out(w):
        return pltpu.make_async_copy(
            dq_ref.at[w], dq_hbm.at[pl.ds(pl.multiple_of(w * window, window), window), :],
            out_sems.at[w],
        )

    def attend(w, prompt_rows):
        first_row = pl.multiple_of(w * window, window)
        band_row = pl.multiple_of(jnp.maximum(first_row - window, 0), window)
        rows = pl.ds(first_row, window)
        cont_rows = pl.ds(band_row, band)
        row = first_row + lax.broadcasted_iota(jnp.int32, (1, lanes), 1) % window
        offset = jnp.zeros((1, lanes), jnp.int32)
        start = jnp.full((1, lanes), windows * window, jnp.int32)
        for c in range(per_device):
            inside = (row >= table[0, c]) & (row < table[1, c])
            offset = jnp.where(inside, table[2, c], offset)
            start = jnp.where(inside, table[0, c], start)
        valid = row < filled
        every = [(i * chunk, chunk) for i in range(prompt_rows // chunk)] + [(prompt_len, band)]
        cont_place = band_row + lax.broadcasted_iota(jnp.int32, (band, lanes), 0)
        cont_seen = (cont_place >= start) & (cont_place <= row)
        head_slices = [slice(h * HEAD_WIDTH, (h + 1) * HEAD_WIDTH) for h in range(heads)]
        ck = [ck_ref[cont_rows, s] for s in head_slices]
        cv = [cv_ref[cont_rows, s] for s in head_slices]
        units = [(h, i) for h in range(heads) for i in range(per_head)]
        state = [dict() for _ in units]

        def rows_of(ref, u):
            h, i = units[u]
            first = h * head_columns + i * group * HEAD_WIDTH
            return jnp.concatenate(
                [
                    ref[rows, first + j * HEAD_WIDTH : first + (j + 1) * HEAD_WIDTH]
                    for j in range(group)
                ],
                axis=0,
            )

        def columns(u):
            return slice(units[u][1] * lanes, (units[u][1] + 1) * lanes)

        def score_chunk(u, n):
            h = units[u][0]
            here = state[u]
            first, size = every[n]
            if n == 0:
                here["q"] = rows_of(q_ref, u)
                here["top"] = jnp.full((8, lanes), MASKED_SCORE, F32)
            k = keys[h, first : first + size] if first < prompt_len else ck[h]
            s = lax.dot_general(k, here["q"], DIMS_NT, preferred_element_type=F32) * factor
            if first == prompt_len:
                s = jnp.where(cont_seen, s, MASKED_SCORE)
            elif first >= half:
                spot = first + lax.broadcasted_iota(jnp.int32, s.shape, 0)
                s = jnp.where(spot < offset, s, MASKED_SCORE)
            score[h, first : first + size, columns(u)] = s
            here["top"] = jnp.maximum(here["top"], fold(s, jnp.max))

        def weight_chunk(u, n):
            h = units[u][0]
            here = state[u]
            first, size = every[n]
            if n == 0:
                here["g"] = rows_of(g_ref, u)
                here["top"] = jnp.max(here["top"], axis=0, keepdims=True)
                here["total"] = jnp.zeros((8, lanes), F32)
                here["delta"] = jnp.zeros((8, lanes), F32)
            v = values[h, first : first + size] if first < prompt_len else cv[h]
            dp = lax.dot_general(v, here["g"], DIMS_NT, preferred_element_type=F32)
            e = jnp.exp2(score[h, first : first + size, columns(u)] - here["top"])
            dprob[h, first : first + size, columns(u)] = dp
            expo[h, first : first + size, columns(u)] = e.astype(BF16)
            here["total"] = here["total"] + fold(e, jnp.sum)
            here["delta"] = here["delta"] + fold(e * dp, jnp.sum)

        def grad_chunk(u, n):
            h = units[u][0]
            here = state[u]
            first, size = every[n]
            if n == 0:
                total = jnp.sum(here["total"], axis=0, keepdims=True)
                inverse = jnp.where(valid, 1.0 / total, 0.0)
                here["inverse"] = inverse
                here["delta"] = jnp.sum(here["delta"], axis=0, keepdims=True) / total
                column = jnp.broadcast_to(inverse, (HEAD_WIDTH, lanes)).T
                here["sq"] = (here["q"].astype(F32) * (column * scale)).astype(BF16)
                here["sg"] = (here["g"].astype(F32) * column).astype(BF16)
            e = expo[h, first : first + size, columns(u)].astype(F32)
            sgrad[h, first : first + size, columns(u)] = (
                e * (dprob[h, first : first + size, columns(u)] - here["delta"])
            ).astype(BF16)

        def sums(h):
            mine = [u for u in range(len(units)) if units[u][0] == h]
            g_all = jnp.concatenate([state[u]["sg"] for u in mine], axis=0)
            q_all = jnp.concatenate([state[u]["sq"] for u in mine], axis=0)
            acc[h, :prompt_rows, HEAD_WIDTH:] += lax.dot_general(
                expo[h, :prompt_rows, :], g_all, DIMS_NN, preferred_element_type=F32
            )
            cacc_v[h, cont_rows, :] += lax.dot_general(
                expo[h, prompt_len:, :], g_all, DIMS_NN, preferred_element_type=F32
            )
            acc[h, :prompt_rows, :HEAD_WIDTH] += lax.dot_general(
                sgrad[h, :prompt_rows, :], q_all, DIMS_NN, preferred_element_type=F32
            )
            cacc_k[h, cont_rows, :] += lax.dot_general(
                sgrad[h, prompt_len:, :], q_all, DIMS_NN, preferred_element_type=F32
            )
            ck_t = ck[h].astype(F32).T.astype(BF16)
            for u in mine:
                dq_t = lax.dot_general(
                    keys_t[h, :, :prompt_rows],
                    sgrad[h, :prompt_rows, columns(u)],
                    DIMS_NN,
                    preferred_element_type=F32,
                ) + lax.dot_general(
                    ck_t, sgrad[h, prompt_len:, columns(u)], DIMS_NN, preferred_element_type=F32
                )
                dq = (dq_t * (state[u]["inverse"] * scale)).T.astype(BF16)
                for j in range(group):
                    first = h * head_columns + (units[u][1] * group + j) * HEAD_WIDTH
                    dq_ref[w, :, first : first + HEAD_WIDTH] = dq[j * window : (j + 1) * window]

        for turn in range(len(units) + 2):
            for n in range(len(every)):
                if turn < len(units):
                    score_chunk(turn, n)
                if 0 <= turn - 1 < len(units):
                    weight_chunk(turn - 1, n)
                if 0 <= turn - 2 < len(units):
                    grad_chunk(turn - 2, n)
            if 0 <= turn - 2 and (turn - 1) % per_head == 0:
                sums(units[turn - 2][0])

    def step(w, carry):
        first_row = w * window
        reach = jnp.int32(0)
        for c in range(per_device):
            meets = (table[0, c] < first_row + window) & (table[1, c] > first_row)
            reach = jnp.maximum(reach, jnp.where(meets, table[2, c], 0))
        level = jnp.where(
            first_row >= filled, levels + 1, (jnp.maximum(reach - half, 0) + grain - 1) // grain
        )
        for n in range(levels + 1):

            @pl.when(level == n)
            def _(n=n):
                attend(w, half + n * grain)

        @pl.when(level == levels + 1)
        def _():
            dq_ref[w] = jnp.zeros(dq_ref.shape[1:], BF16)

        copy_out(w).start()
        return carry

    lax.fori_loop(0, windows, step, jnp.int32(0))
    for h in range(heads):
        here = slice(h * HEAD_WIDTH, (h + 1) * HEAD_WIDTH)
        dck_ref[:, here] = cacc_k[h].astype(BF16)
        dcv_ref[:, here] = cacc_v[h].astype(BF16)
    for ref, core in ((send_ref, 1 - my_core), (keep_ref, my_core)):
        for q in range(prefix_count):
            for z in range(chips):
                for h in range(heads):
                    block = acc[h, pl.ds(token_base(q, z, core), own_rows), :].astype(BF16)
                    here = slice(h * HEAD_WIDTH, (h + 1) * HEAD_WIDTH)
                    ref[q * chips + z, :, here] = block[:, :HEAD_WIDTH]
                    there = slice(width + h * HEAD_WIDTH, width + (h + 1) * HEAD_WIDTH)
                    ref[q * chips + z, :, there] = block[:, HEAD_WIDTH:]
    for w in range(windows):
        copy_out(w).wait()


def attention(
    where, assign, lengths, offsets, own, other, query, grad_out, cont_key, cont_value, axes
):
    prefix_count, cand_count = axes
    rows, query_width = query.shape
    heads = cont_key.shape[1] // HEAD_WIDTH
    head_columns = query_width // heads
    per_device = assign.shape[0] // cand_count
    window = rows // per_device
    piece_width = own.shape[2]
    prompt_len = 2 * own.shape[0] * own.shape[1]
    group = min(max(256 // window, 1), head_columns // HEAD_WIDTH)
    all_lanes = head_columns // HEAD_WIDTH * window
    joined = prompt_len + 2 * window

    return pl.pallas_call(
        functools.partial(
            attention_body, prefix_count, cand_count, window, per_device, heads, group
        ),
        in_specs=[smem_spec()] * 4 + [vmem_spec()] * 6,
        out_specs=[pl.BlockSpec(memory_space=pl.ANY)] + [vmem_spec()] * 4,
        scratch_shapes=[
            pltpu.SMEM((3, per_device + 1), jnp.int32),
            pltpu.VMEM((prompt_len, piece_width), F32),
            pltpu.VMEM((heads, prompt_len, HEAD_WIDTH), BF16),
            pltpu.VMEM((heads, prompt_len, HEAD_WIDTH), BF16),
            pltpu.VMEM((heads, HEAD_WIDTH, prompt_len), BF16),
            pltpu.VMEM((per_device, window, query_width), BF16),
            pltpu.VMEM((heads, joined, all_lanes), F32),
            pltpu.VMEM((heads, joined, all_lanes), F32),
            pltpu.VMEM((heads, joined, all_lanes), BF16),
            pltpu.VMEM((heads, joined, all_lanes), BF16),
            pltpu.VMEM((heads, prompt_len, 2 * HEAD_WIDTH), F32),
            pltpu.VMEM((heads, rows, HEAD_WIDTH), F32),
            pltpu.VMEM((heads, rows, HEAD_WIDTH), F32),
            pltpu.SemaphoreType.DMA((per_device,)),
        ],
        out_shape=[
            jax.ShapeDtypeStruct(query.shape, BF16),
            jax.ShapeDtypeStruct(cont_key.shape, BF16),
            jax.ShapeDtypeStruct(cont_value.shape, BF16),
            jax.ShapeDtypeStruct(own.shape, BF16),
            jax.ShapeDtypeStruct(own.shape, BF16),
        ],
        compiler_params=pltpu.CompilerParams(vmem_limit_bytes=VMEM_BYTES),
        cost_estimate=pl.CostEstimate(
            flops=10 * query.size * joined,
            bytes_accessed=8 * query.size,
            transcendentals=query.size * 4,
        ),
        name="attention_backward",
    )(
        where,
        assign,
        lengths,
        offsets,
        own,
        other,
        cont_key,
        cont_value,
        query,
        grad_out,
    )


def per_device(
    query,
    grad_out,
    continuation_key,
    continuation_value,
    prompt_key,
    shared_prompt_value,
    assign,
    lengths,
    offsets,
):
    prefix_count = lax.axis_size("prefix")
    cand_count = lax.axis_size("cand")
    chips = cand_count // 2
    where = jnp.reshape(lax.axis_index("cand"), (1,)).astype(jnp.int32)
    same_core = [
        [p * cand_count + 2 * z + core for p in range(prefix_count) for z in range(chips)]
        for core in range(2)
    ]

    def exchange(x):
        return lax.all_to_all(
            x, ("prefix", "cand"), 0, 0, tiled=True, axis_index_groups=same_core
        )

    def to_sibling(x):
        return lax.ppermute(x, "cand", [(i, i ^ 1) for i in range(cand_count)])

    own = exchange(split_heads(prompt_key, shared_prompt_value, prefix_count, chips))
    query_grad, cont_key_grad, cont_value_grad, kept, sent = attention(
        where,
        assign,
        lengths,
        offsets,
        own,
        to_sibling(own),
        query,
        grad_out,
        continuation_key,
        continuation_value,
        (prefix_count, cand_count),
    )
    by_chip = exchange(add_sibling(kept, to_sibling(sent)))
    prompt_key_grad, prompt_value_grad = add_chips(by_chip, prefix_count, chips)
    return (query_grad, cont_key_grad, cont_value_grad, prompt_key_grad, prompt_value_grad)


def solution(mesh):
    in_specs = (
        P("cand", "prefix"),
        P("cand", "prefix"),
        P("cand", "prefix"),
        P("cand", "prefix"),
        P(("prefix", "cand"), None),
        P(("prefix", "cand"), None),
        P(),
        P(),
        P(),
    )
    out_specs = (
        P("cand", "prefix"),
        P("cand", "prefix"),
        P("cand", "prefix"),
        P(("prefix", "cand"), None),
        P(("prefix", "cand"), None),
    )
    return jax.shard_map(
        per_device, mesh=mesh, in_specs=in_specs, out_specs=out_specs, check_vma=False
    )
```

```python
import functools
import math

import jax
import jax.numpy as jnp
from jax import lax
from jax.experimental import pallas as pl
from jax.experimental.pallas import tpu as pltpu
from jax.sharding import PartitionSpec as P

HEAD_WIDTH = 128
MASKED_SCORE = -1e30
F32 = jnp.float32
BF16 = jnp.bfloat16
VMEM_BYTES = 40 * 1024 * 1024
GLUE_VMEM_BYTES = 8 * 1024 * 1024
DIMS_NT = (((1,), (1,)), ((), ()))
DIMS_NN = (((1,), (0,)), ((), ()))


def vmem_spec():
    return pl.BlockSpec(memory_space=pltpu.VMEM)


def smem_spec():
    return pl.BlockSpec(memory_space=pltpu.SMEM)


def glue_call(body, out_shape, operands, scalars=1, name=None):
    return pl.pallas_call(
        body,
        out_shape=out_shape,
        in_specs=[smem_spec()] * scalars + [vmem_spec()] * (len(operands) - scalars),
        out_specs=[vmem_spec()] * len(out_shape),
        compiler_params=pltpu.CompilerParams(vmem_limit_bytes=GLUE_VMEM_BYTES),
        name=name,
    )(*operands)


TOKEN = (8, HEAD_WIDTH)


def split_heads(joined, parts, chips):
    rows, double = joined.shape
    full = double // 2
    width = full // parts

    def body(joined_ref, out_ref, token_ref):
        for q in range(parts):
            first = q * width
            key = joined_ref[:, first : first + width]
            value = joined_ref[:, full + first : full + first + width]
            for z in range(chips):
                out_ref[q * chips + z, :, :width] = key
                out_ref[q * chips + z, :, width:] = value
        token_ref[...] = jnp.zeros(TOKEN, F32)

    shapes = [
        jax.ShapeDtypeStruct((parts * chips, rows, 2 * width), BF16),
        jax.ShapeDtypeStruct(TOKEN, F32),
    ]
    return glue_call(body, shapes, (joined,), scalars=0, name="split_heads")


def tie(x, token):
    def body(x_ref, token_ref, out_ref):
        del x_ref, token_ref, out_ref

    hbm = pl.BlockSpec(memory_space=pl.ANY)
    return pl.pallas_call(
        body,
        out_shape=jax.ShapeDtypeStruct(x.shape, x.dtype),
        in_specs=[hbm, vmem_spec()],
        out_specs=hbm,
        input_output_aliases={0: 0},
        compiler_params=pltpu.CompilerParams(vmem_limit_bytes=GLUE_VMEM_BYTES),
        name="tie",
    )(x, token)


def stage_rows(token, arrays):
    count = len(arrays)

    def body(token_ref, *refs):
        sems = refs[-1]
        refs[2 * count][...] = token_ref[...]
        copies = [
            pltpu.make_async_copy(refs[i], refs[count + i], sems.at[i]) for i in range(count)
        ]
        for copy in copies:
            copy.start()
        for copy in copies:
            copy.wait()

    return pl.pallas_call(
        body,
        out_shape=[jax.ShapeDtypeStruct(x.shape, x.dtype) for x in (*arrays, token)],
        in_specs=[vmem_spec()] + [pl.BlockSpec(memory_space=pl.ANY)] * count,
        out_specs=[vmem_spec()] * (count + 1),
        scratch_shapes=[pltpu.SemaphoreType.DMA((count,))],
        compiler_params=pltpu.CompilerParams(vmem_limit_bytes=GLUE_VMEM_BYTES),
        cost_estimate=pl.CostEstimate(
            flops=0, bytes_accessed=4 * sum(x.size for x in arrays), transcendentals=0
        ),
        name="stage_rows",
    )(token, *arrays)


def add_sibling(kept, arrived):
    def body(kept_ref, arrived_ref, out_ref, token_ref):
        for i in range(kept.shape[0]):
            out_ref[i] = (kept_ref[i].astype(F32) + arrived_ref[i].astype(F32)).astype(BF16)
        token_ref[...] = jnp.zeros(TOKEN, F32)

    shapes = [jax.ShapeDtypeStruct(kept.shape, BF16), jax.ShapeDtypeStruct(TOKEN, F32)]
    return glue_call(body, shapes, (kept, arrived), scalars=0, name="add_sibling")


def add_chips(pieces, parts, chips):
    rows, double = pieces.shape[1:]
    width = double // 2

    def body(piece_ref, key_ref, value_ref):
        for p in range(parts):
            total = piece_ref[p * chips].astype(F32)
            for z in range(1, chips):
                total = total + piece_ref[p * chips + z].astype(F32)
            total = total.astype(BF16)
            key_ref[:, p * width : (p + 1) * width] = total[:, :width]
            value_ref[:, p * width : (p + 1) * width] = total[:, width:]

    shapes = [jax.ShapeDtypeStruct((rows, width * parts), BF16)] * 2
    return glue_call(body, shapes, (pieces,), scalars=0, name="add_chips")


def fill_table(table, cand, assign_ref, lengths_ref, offsets_ref):
    count, place = jnp.int32(0), jnp.int32(0)
    for k in range(assign_ref.shape[0]):
        length = lengths_ref[k]
        table[0, count] = place
        table[1, count] = place + length
        table[2, count] = offsets_ref[k]
        mine = (assign_ref[k] == cand).astype(jnp.int32)
        count = count + mine
        place = place + mine * length
    return place


def level_of(table, filled, w, window, per_device, half, grain, levels):
    first_row = w * window
    reach = jnp.int32(0)
    for c in range(per_device):
        meets = (table[0, c] < first_row + window) & (table[1, c] > first_row)
        reach = jnp.maximum(reach, jnp.where(meets, table[2, c], 0))
    return jnp.where(
        first_row >= filled, levels + 1, (jnp.maximum(reach - half, 0) + grain - 1) // grain
    )


def fold(x, op):
    return op(x.reshape(x.shape[0] // 8, 8, x.shape[1]), axis=0)


def query_body(
    window,
    per_device,
    heads,
    group,
    where_ref,
    assign_ref,
    lengths_ref,
    offsets_ref,
    joint_ref,
    stat_ref,
    ck_ref,
    cv_ref,
    q_ref,
    g_ref,
    token_ref,
    dq_hbm,
    table,
    keys_t,
    sgrad,
    dq_ref,
    out_sems,
):
    del token_ref
    windows = per_device
    prompt_len = joint_ref.shape[0]
    half = prompt_len // 2
    levels = 3 if half % (3 * 128) == 0 else 1
    grain = half // levels
    chunk = math.gcd(half, 128)
    band = 2 * window
    lanes = group * window
    head_columns = q_ref.shape[1] // heads
    per_head = head_columns // HEAD_WIDTH // group
    scale = 1.0 / math.sqrt(HEAD_WIDTH)
    factor = scale * math.log2(math.e)
    width = heads * HEAD_WIDTH
    filled = fill_table(table, where_ref[0], assign_ref, lengths_ref, offsets_ref)
    for h in range(heads):
        block = joint_ref[:, h * HEAD_WIDTH : (h + 1) * HEAD_WIDTH]
        keys_t[h] = block.astype(F32).T.astype(BF16)

    def copy_out(w):
        rows = pl.ds(pl.multiple_of(w * window, window), window)
        return pltpu.make_async_copy(dq_ref.at[w], dq_hbm.at[rows, :], out_sems.at[w])

    def attend(w, prompt_rows):
        first_row = pl.multiple_of(w * window, window)
        band_row = pl.multiple_of(jnp.maximum(first_row - window, 0), window)
        rows = pl.ds(first_row, window)
        cont_rows = pl.ds(band_row, band)
        row = first_row + lax.broadcasted_iota(jnp.int32, (1, lanes), 1) % window
        offset = jnp.zeros((1, lanes), jnp.int32)
        start = jnp.full((1, lanes), windows * window, jnp.int32)
        for c in range(per_device):
            inside = (row >= table[0, c]) & (row < table[1, c])
            offset = jnp.where(inside, table[2, c], offset)
            start = jnp.where(inside, table[0, c], start)
        every = [(i * chunk, chunk) for i in range(prompt_rows // chunk)] + [(prompt_len, band)]
        cont_place = band_row + lax.broadcasted_iota(jnp.int32, (band, lanes), 0)
        cont_seen = (cont_place >= start) & (cont_place <= row)
        units = [(h, i) for h in range(heads) for i in range(per_head)]
        for u, (h, i) in enumerate(units):
            base = h * head_columns + i * group * HEAD_WIDTH
            places = [slice(base + j * HEAD_WIDTH, base + (j + 1) * HEAD_WIDTH) for j in range(group)]
            q = jnp.concatenate([q_ref[rows, p] for p in places], axis=0)
            g = jnp.concatenate([g_ref[rows, p] for p in places], axis=0)
            here = slice(h * HEAD_WIDTH, (h + 1) * HEAD_WIDTH)
            there = slice(width + here.start, width + here.stop)
            ck = ck_ref[cont_rows, here]
            cv = cv_ref[cont_rows, here]
            top = stat_ref[w, u, 0:1, :]
            inverse = stat_ref[w, u, 2:3, :]
            delta = stat_ref[w, u, 4:5, :]
            for first, size in every:
                part = slice(first, first + size)
                k = joint_ref[part, here] if first < prompt_len else ck
                v = joint_ref[part, there] if first < prompt_len else cv
                s = lax.dot_general(k, q, DIMS_NT, preferred_element_type=F32) * factor
                if first == prompt_len:
                    s = jnp.where(cont_seen, s, MASKED_SCORE)
                elif first >= half:
                    spot = first + lax.broadcasted_iota(jnp.int32, s.shape, 0)
                    s = jnp.where(spot < offset, s, MASKED_SCORE)
                dp = lax.dot_general(v, g, DIMS_NT, preferred_element_type=F32)
                sgrad[u, part, :] = (jnp.exp2(s - top) * (dp - delta)).astype(BF16)
            dq_t = lax.dot_general(
                keys_t[h, :, :prompt_rows],
                sgrad[u, :prompt_rows, :],
                DIMS_NN,
                preferred_element_type=F32,
            ) + lax.dot_general(
                ck.astype(F32).T.astype(BF16),
                sgrad[u, prompt_len:, :],
                DIMS_NN,
                preferred_element_type=F32,
            )
            dq = (dq_t * (inverse * scale)).T.astype(BF16)
            for j, p in enumerate(places):
                dq_ref[w, :, p] = dq[j * window : (j + 1) * window]

    def step(w, carry):
        level = level_of(table, filled, w, window, per_device, half, grain, levels)
        for n in range(levels + 1):

            @pl.when(level == n)
            def _(n=n):
                attend(w, half + n * grain)

        @pl.when(level == levels + 1)
        def _():
            dq_ref[w] = jnp.zeros(dq_ref.shape[1:], BF16)

        copy_out(w).start()
        return carry

    lax.fori_loop(0, windows, step, jnp.int32(0))
    for w in range(windows):
        copy_out(w).wait()


def attention_body(
    prefix_count,
    cand_count,
    window,
    per_device,
    heads,
    group,
    where_ref,
    assign_ref,
    lengths_ref,
    offsets_ref,
    own_ref,
    other_ref,
    ck_ref,
    cv_ref,
    q_ref,
    g_ref,
    joint_ref,
    stat_ref,
    dck_ref,
    dcv_ref,
    keep_ref,
    send_ref,
    table,
    stage,
    score,
    dprob,
    expo,
    sgrad,
    acc,
    cacc_k,
    cacc_v,
):
    chips = cand_count // 2
    own_rows = own_ref.shape[1]
    windows = per_device
    prompt_len = joint_ref.shape[0]
    half = prompt_len // 2
    levels = 3 if half % (3 * 128) == 0 else 1
    grain = half // levels
    chunk = math.gcd(half, 128)
    band = 2 * window
    lanes = group * window
    head_columns = q_ref.shape[1] // heads
    per_head = head_columns // HEAD_WIDTH // group
    scale = 1.0 / math.sqrt(HEAD_WIDTH)
    factor = scale * math.log2(math.e)
    width = heads * HEAD_WIDTH
    my_cand = where_ref[0]
    my_core = lax.rem(my_cand, 2)

    filled = fill_table(table, my_cand, assign_ref, lengths_ref, offsets_ref)

    def token_base(q, z, core):
        return pl.multiple_of((q * cand_count + 2 * z + core) * own_rows, 8)

    for ref, core in ((own_ref, my_core), (other_ref, 1 - my_core)):
        for q in range(prefix_count):
            for z in range(chips):
                stage[pl.ds(token_base(q, z, core), own_rows), :] = ref[q * chips + z].astype(F32)
    joint_ref[...] = stage[...].astype(BF16)
    acc[...] = jnp.zeros_like(acc)
    cacc_k[...] = jnp.zeros_like(cacc_k)
    cacc_v[...] = jnp.zeros_like(cacc_v)

    def attend(w, prompt_rows):
        first_row = pl.multiple_of(w * window, window)
        band_row = pl.multiple_of(jnp.maximum(first_row - window, 0), window)
        rows = pl.ds(first_row, window)
        cont_rows = pl.ds(band_row, band)
        row = first_row + lax.broadcasted_iota(jnp.int32, (1, lanes), 1) % window
        offset = jnp.zeros((1, lanes), jnp.int32)
        start = jnp.full((1, lanes), windows * window, jnp.int32)
        for c in range(per_device):
            inside = (row >= table[0, c]) & (row < table[1, c])
            offset = jnp.where(inside, table[2, c], offset)
            start = jnp.where(inside, table[0, c], start)
        valid = row < filled
        every = [(i * chunk, chunk) for i in range(prompt_rows // chunk)] + [(prompt_len, band)]
        cont_place = band_row + lax.broadcasted_iota(jnp.int32, (band, lanes), 0)
        cont_seen = (cont_place >= start) & (cont_place <= row)
        head_slices = [slice(h * HEAD_WIDTH, (h + 1) * HEAD_WIDTH) for h in range(heads)]
        value_slices = [slice(width + s.start, width + s.stop) for s in head_slices]
        ck = [ck_ref[cont_rows, s] for s in head_slices]
        cv = [cv_ref[cont_rows, s] for s in head_slices]
        units = [(h, i) for h in range(heads) for i in range(per_head)]
        state = [dict() for _ in units]

        def rows_of(ref, u):
            h, i = units[u]
            first = h * head_columns + i * group * HEAD_WIDTH
            return jnp.concatenate(
                [
                    ref[rows, first + j * HEAD_WIDTH : first + (j + 1) * HEAD_WIDTH]
                    for j in range(group)
                ],
                axis=0,
            )

        def columns(u):
            return slice(units[u][1] * lanes, (units[u][1] + 1) * lanes)

        def score_chunk(u, n):
            h = units[u][0]
            here = state[u]
            first, size = every[n]
            if n == 0:
                here["q"] = rows_of(q_ref, u)
                here["top"] = jnp.full((8, lanes), MASKED_SCORE, F32)
            k = joint_ref[first : first + size, head_slices[h]] if first < prompt_len else ck[h]
            s = lax.dot_general(k, here["q"], DIMS_NT, preferred_element_type=F32) * factor
            if first == prompt_len:
                s = jnp.where(cont_seen, s, MASKED_SCORE)
            elif first >= half:
                spot = first + lax.broadcasted_iota(jnp.int32, s.shape, 0)
                s = jnp.where(spot < offset, s, MASKED_SCORE)
            score[h, first : first + size, columns(u)] = s
            here["top"] = jnp.maximum(here["top"], fold(s, jnp.max))

        def weight_chunk(u, n):
            h = units[u][0]
            here = state[u]
            first, size = every[n]
            if n == 0:
                here["g"] = rows_of(g_ref, u)
                here["top"] = jnp.max(here["top"], axis=0, keepdims=True)
                here["total"] = jnp.zeros((8, lanes), F32)
                here["delta"] = jnp.zeros((8, lanes), F32)
            v = joint_ref[first : first + size, value_slices[h]] if first < prompt_len else cv[h]
            dp = lax.dot_general(v, here["g"], DIMS_NT, preferred_element_type=F32)
            e = jnp.exp2(score[h, first : first + size, columns(u)] - here["top"])
            dprob[h, first : first + size, columns(u)] = dp.astype(BF16)
            expo[h, first : first + size, columns(u)] = e.astype(BF16)
            here["total"] = here["total"] + fold(e, jnp.sum)
            here["delta"] = here["delta"] + fold(e * dp, jnp.sum)

        def grad_chunk(u, n):
            h = units[u][0]
            here = state[u]
            first, size = every[n]
            if n == 0:
                total = jnp.sum(here["total"], axis=0, keepdims=True)
                inverse = jnp.where(valid, 1.0 / total, 0.0)
                delta = jnp.sum(here["delta"], axis=0, keepdims=True) / total
                stats = (here["top"], inverse, delta, delta)
                stat_ref[w, u] = jnp.concatenate(
                    [jnp.broadcast_to(x, (2, lanes)) for x in stats], axis=0
                )
                tall = max(chunk, band)
                here["delta"] = jnp.broadcast_to(delta, (tall, lanes)).astype(BF16)
                column = jnp.broadcast_to(inverse, (HEAD_WIDTH, lanes)).T
                here["sq"] = (here["q"].astype(F32) * (column * scale)).astype(BF16)
                here["sg"] = (here["g"].astype(F32) * column).astype(BF16)
            part = slice(first, first + size)
            sgrad[h, part, columns(u)] = expo[h, part, columns(u)] * (
                dprob[h, part, columns(u)] - here["delta"][:size]
            )

        def sums(h):
            mine = [u for u in range(len(units)) if units[u][0] == h]
            g_all = jnp.concatenate([state[u]["sg"] for u in mine], axis=0)
            q_all = jnp.concatenate([state[u]["sq"] for u in mine], axis=0)
            acc[h, :prompt_rows, HEAD_WIDTH:] += lax.dot_general(
                expo[h, :prompt_rows, :], g_all, DIMS_NN, preferred_element_type=F32
            )
            cacc_v[h, cont_rows, :] += lax.dot_general(
                expo[h, prompt_len:, :], g_all, DIMS_NN, preferred_element_type=F32
            )
            acc[h, :prompt_rows, :HEAD_WIDTH] += lax.dot_general(
                sgrad[h, :prompt_rows, :], q_all, DIMS_NN, preferred_element_type=F32
            )
            cacc_k[h, cont_rows, :] += lax.dot_general(
                sgrad[h, prompt_len:, :], q_all, DIMS_NN, preferred_element_type=F32
            )

        for turn in range(len(units) + 2):
            for n in range(len(every)):
                if turn < len(units):
                    score_chunk(turn, n)
                if 0 <= turn - 1 < len(units):
                    weight_chunk(turn - 1, n)
                if 0 <= turn - 2 < len(units):
                    grad_chunk(turn - 2, n)
            if 0 <= turn - 2 and (turn - 1) % per_head == 0:
                sums(units[turn - 2][0])

    def step(w, carry):
        level = level_of(table, filled, w, window, per_device, half, grain, levels)
        for n in range(levels + 1):

            @pl.when(level == n)
            def _(n=n):
                attend(w, half + n * grain)

        return carry

    lax.fori_loop(0, windows, step, jnp.int32(0))
    for h in range(heads):
        here = slice(h * HEAD_WIDTH, (h + 1) * HEAD_WIDTH)
        dck_ref[:, here] = cacc_k[h].astype(BF16)
        dcv_ref[:, here] = cacc_v[h].astype(BF16)
    for ref, core in ((send_ref, 1 - my_core), (keep_ref, my_core)):
        for q in range(prefix_count):
            for z in range(chips):
                for h in range(heads):
                    block = acc[h, pl.ds(token_base(q, z, core), own_rows), :].astype(BF16)
                    here = slice(h * HEAD_WIDTH, (h + 1) * HEAD_WIDTH)
                    ref[q * chips + z, :, here] = block[:, :HEAD_WIDTH]
                    there = slice(width + h * HEAD_WIDTH, width + (h + 1) * HEAD_WIDTH)
                    ref[q * chips + z, :, there] = block[:, HEAD_WIDTH:]


def attention(
    where, assign, lengths, offsets, own, other, query, grad_out, cont_key, cont_value, axes
):
    prefix_count, cand_count = axes
    rows, query_width = query.shape
    heads = cont_key.shape[1] // HEAD_WIDTH
    head_columns = query_width // heads
    per_device = assign.shape[0] // cand_count
    window = rows // per_device
    piece_width = own.shape[2]
    prompt_len = 2 * own.shape[0] * own.shape[1]
    group = min(max(256 // window, 1), head_columns // HEAD_WIDTH)
    all_lanes = head_columns // HEAD_WIDTH * window
    joined = prompt_len + 2 * window

    units = heads * (head_columns // HEAD_WIDTH // group)
    scalars = (where, assign, lengths, offsets)
    hbm = pl.BlockSpec(memory_space=pl.ANY)
    joint, stats, dck, dcv, keep, send = pl.pallas_call(
        functools.partial(
            attention_body, prefix_count, cand_count, window, per_device, heads, group
        ),
        in_specs=[smem_spec()] * 4 + [vmem_spec()] * 6,
        out_specs=[vmem_spec()] * 6,
        scratch_shapes=[
            pltpu.SMEM((3, per_device + 1), jnp.int32),
            pltpu.VMEM((prompt_len, piece_width), F32),
            pltpu.VMEM((heads, joined, all_lanes), F32),
            pltpu.VMEM((heads, joined, all_lanes), BF16),
            pltpu.VMEM((heads, joined, all_lanes), BF16),
            pltpu.VMEM((heads, joined, all_lanes), BF16),
            pltpu.VMEM((heads, prompt_len, 2 * HEAD_WIDTH), F32),
            pltpu.VMEM((heads, rows, HEAD_WIDTH), F32),
            pltpu.VMEM((heads, rows, HEAD_WIDTH), F32),
        ],
        out_shape=[
            jax.ShapeDtypeStruct((prompt_len, piece_width), BF16),
            jax.ShapeDtypeStruct((per_device, units, 8, group * window), F32),
            jax.ShapeDtypeStruct(cont_key.shape, BF16),
            jax.ShapeDtypeStruct(cont_value.shape, BF16),
            jax.ShapeDtypeStruct(own.shape, BF16),
            jax.ShapeDtypeStruct(own.shape, BF16),
        ],
        compiler_params=pltpu.CompilerParams(vmem_limit_bytes=VMEM_BYTES),
        cost_estimate=pl.CostEstimate(
            flops=8 * query.size * joined,
            bytes_accessed=8 * query.size,
            transcendentals=query.size * 4,
        ),
        name="attention_sums",
    )(*scalars, own, other, cont_key, cont_value, query, grad_out)

    def finish(token):
        return pl.pallas_call(
            functools.partial(query_body, window, per_device, heads, group),
            in_specs=[smem_spec()] * 4 + [vmem_spec()] * 7,
            out_specs=hbm,
            scratch_shapes=[
                pltpu.SMEM((3, per_device + 1), jnp.int32),
                pltpu.VMEM((heads, HEAD_WIDTH, prompt_len), BF16),
                pltpu.VMEM((units, joined, group * window), BF16),
                pltpu.VMEM((per_device, window, query_width), BF16),
                pltpu.SemaphoreType.DMA((per_device,)),
            ],
            out_shape=jax.ShapeDtypeStruct(query.shape, BF16),
            compiler_params=pltpu.CompilerParams(vmem_limit_bytes=VMEM_BYTES // 2),
            cost_estimate=pl.CostEstimate(
                flops=6 * query.size * joined,
                bytes_accessed=8 * query.size,
                transcendentals=query.size * 4,
            ),
            name="attention_query",
        )(*scalars, joint, stats, cont_key, cont_value, query, grad_out, token)

    return finish, dck, dcv, keep, send


def per_device(
    query,
    grad_out,
    continuation_key,
    continuation_value,
    prompt_key,
    shared_prompt_value,
    assign,
    lengths,
    offsets,
):
    prefix_count = lax.axis_size("prefix")
    cand_count = lax.axis_size("cand")
    chips = cand_count // 2
    where = jnp.reshape(lax.axis_index("cand"), (1,)).astype(jnp.int32)
    same_core = [
        [p * cand_count + 2 * z + core for p in range(prefix_count) for z in range(chips)]
        for core in range(2)
    ]

    def exchange(x):
        return lax.all_to_all(
            x, ("prefix", "cand"), 0, 0, tiled=True, axis_index_groups=same_core
        )

    def to_sibling(x):
        return lax.ppermute(x, "cand", [(i, i ^ 1) for i in range(cand_count)])

    joined = jnp.concatenate([prompt_key, shared_prompt_value], axis=1)
    pieces, token = split_heads(joined, prefix_count, chips)
    own = exchange(pieces)
    query, grad_out, continuation_key, continuation_value, token = stage_rows(
        token, (query, grad_out, continuation_key, continuation_value)
    )
    own = tie(own, token)
    finish, cont_key_grad, cont_value_grad, kept, sent = attention(
        where,
        assign,
        lengths,
        offsets,
        own,
        to_sibling(own),
        query,
        grad_out,
        continuation_key,
        continuation_value,
        (prefix_count, cand_count),
    )
    summed, token = add_sibling(kept, to_sibling(sent))
    by_chip = exchange(summed)
    query_grad = finish(token)
    prompt_key_grad, prompt_value_grad = add_chips(by_chip, prefix_count, chips)
    return (query_grad, cont_key_grad, cont_value_grad, prompt_key_grad, prompt_value_grad)


def solution(mesh):
    in_specs = (
        P("cand", "prefix"),
        P("cand", "prefix"),
        P("cand", "prefix"),
        P("cand", "prefix"),
        P(("prefix", "cand"), None),
        P(("prefix", "cand"), None),
        P(),
        P(),
        P(),
    )
    out_specs = (
        P("cand", "prefix"),
        P("cand", "prefix"),
        P("cand", "prefix"),
        P(("prefix", "cand"), None),
        P(("prefix", "cand"), None),
    )
    return jax.shard_map(
        per_device, mesh=mesh, in_specs=in_specs, out_specs=out_specs, check_vma=False
    )
```
